32 devices in a mesh: dp: 8 (over z, x), tensor: 4 (over y, core).
Axes of the slice: x: 2, y: 2, z: 4, core: 2. Of those that a mesh axis runs over, the one named last changes fastest.
Arguments:
- hidden_in: bfloat16 [16384, 640], P('dp'), may hold values from -6 to 6
- query_weight: bfloat16 [640, 1024], P(None, 'tensor'), may hold values from -0.25 to 0.25
- key_weight: bfloat16 [640, 256], replicated, may hold values from -0.25 to 0.25
- value_weight: bfloat16 [640, 256], replicated, may hold values from -0.25 to 0.25
- output_weight: bfloat16 [1024, 640], P('tensor'), may hold values from -0.1875 to 0.1875
- gate_weight: bfloat16 [640, 2048], P(None, 'tensor'), may hold values from -0.25 to 0.25
- up_weight: bfloat16 [640, 2048], P(None, 'tensor'), may hold values from -0.25 to 0.25
- down_weight: bfloat16 [2048, 640], P('tensor'), may hold values from -0.125 to 0.125
- pre_attention: float32 [640], replicated, may hold values from -0.5 to 0.5
- query_norm: float32 [256], replicated, may hold values from -0.5 to 0.5
- key_norm: float32 [256], replicated, may hold values from -0.5 to 0.5
- post_attention: float32 [640], replicated, may hold values from -0.5 to 0.5
- pre_feedforward: float32 [640], replicated, may hold values from -0.5 to 0.5
- post_feedforward: float32 [640], replicated, may hold values from -0.5 to 0.5
- segments: int32 [16384], P('dp'), may hold values from 0 to 15, as said below
- positions: int32 [16384], P('dp'), may hold values from 0 to 511, as said below
- cotangent: bfloat16 [16384, 640], P('dp'), may hold values from -6 to 6
Outputs:
- hidden_out: bfloat16 [16384, 640], P('dp')
- grad_input: float32 [16384, 640], P('dp')
- grad_query_weight: float32 [640, 1024], P(None, 'tensor')
- grad_key_weight: float32 [640, 256], replicated
- grad_value_weight: float32 [640, 256], replicated
- grad_output_weight: float32 [1024, 640], P('tensor')
- grad_gate_weight: float32 [640, 2048], P(None, 'tensor')
- grad_up_weight: float32 [640, 2048], P(None, 'tensor')
- grad_down_weight: float32 [2048, 640], P('tensor')
- grad_pre_attention: float32 [640], replicated
- grad_query_norm: float32 [256], replicated
- grad_key_norm: float32 [256], replicated
- grad_post_attention: float32 [640], replicated
- grad_pre_feedforward: float32 [640], replicated
- grad_post_feedforward: float32 [640], replicated
The draws below stay inside these ranges and needn't reach their ends.
Inputs may be any that keep to these rules, and one draw needn't show every extreme that they name: `segments`: within each aligned block of 512 tokens the document numbers start at 0 at the block's first token and rise by 0 or 1 from one token to the next. `positions`: each token's position is its distance from the first token of its document in the same block.
All inputs are finite; a program needn't handle non-finite values.
Results may differ from the reference program's by a relative error of at most 0.02.
Values may be sent and summed in bfloat16 or wider, within the bound.
A program may use at most 128 MiB of HBM per device.

```python
import jax
import jax.numpy as jnp
from jax import lax

D = 640
HEADS = 4
HEAD_DIM = 256
FF = 2048
LEN = 512
TOKENS = 16384


segment_cap = 15


def pack_layout(key):
    block_count = TOKENS // LEN
    coin_flips = jax.random.randint(jax.random.fold_in(key, 11), (block_count, LEN), 0, LEN // 4)
    single_block = jax.random.randint(jax.random.fold_in(key, 12), (), 0, block_count)
    dense_block = (single_block + 1) % block_count
    blocks = jnp.arange(block_count, dtype=jnp.int32)[:, None]
    offsets = jnp.arange(LEN, dtype=jnp.int32)[None, :]
    starts = (coin_flips == 0) | (offsets == 0)
    starts = starts | (blocks == dense_block) & (offsets % (LEN // 16) == 0)
    starts = jnp.where(blocks == single_block, offsets == 0, starts)
    segment_ids = jnp.minimum(jnp.cumsum(starts.astype(jnp.int32), axis=1) - 1, segment_cap)
    previous = jnp.concatenate([jnp.full((block_count, 1), -1, jnp.int32), segment_ids[:, :-1]], axis=1)
    real_starts = segment_ids != previous
    last_start = lax.cummax(jnp.where(real_starts, offsets, 0), axis=1)
    return (segment_ids.reshape(TOKENS), (offsets - last_start).reshape(TOKENS))


def draw_segments(key, part):
    return pack_layout(key)[0]


def draw_positions(key, part):
    return pack_layout(key)[1]


def shard_levels(rng, dims, split, smallest, largest):
    def one(axis_at, blocks):
        heights = jax.random.uniform(jax.random.fold_in(jax.random.fold_in(rng, 6), axis_at), (blocks,), jnp.float32, smallest / len(split), largest / len(split))
        return jnp.repeat(jnp.exp(heights), dims[axis_at] // blocks).reshape((-1,) + (1,) * (len(dims) - axis_at - 1))

    factor_of = one(*split[0])
    for cut in split[1:]:
        factor_of = factor_of * one(*cut)
    return factor_of


def bell_draw(own_key, extent, width, limit, split=(), kind=jnp.bfloat16):
    entries = jax.random.normal(own_key, extent, jnp.float32) * width
    if len(split) > 0:
        entries = shard_levels(own_key, extent, split, -0.22, 0.18) * entries
    return jnp.clip(entries, min=-limit, max=limit).astype(kind)


def setup_inputs(seed: int = 0) -> dict:
    key_of = jax.random.split(jax.random.key(seed), 18)
    return {
        "hidden_in": bell_draw(key_of[0], (TOKENS, D), 1.0, 6.0, ((0, 8),)),
        "query_weight": bell_draw(key_of[1], (D, HEADS * HEAD_DIM), D ** -0.5, 0.25, ((1, 4),)),
        "key_weight": bell_draw(key_of[2], (D, HEAD_DIM), D ** -0.5, 0.25),
        "value_weight": bell_draw(key_of[3], (D, HEAD_DIM), D ** -0.5, 0.25),
        "output_weight": bell_draw(key_of[4], (HEADS * HEAD_DIM, D), (HEADS * HEAD_DIM) ** -0.5, 0.1875, ((0, 4),)),
        "gate_weight": bell_draw(key_of[5], (D, FF), D ** -0.5, 0.25, ((1, 4),)),
        "up_weight": bell_draw(key_of[6], (D, FF), D ** -0.5, 0.25, ((1, 4),)),
        "down_weight": bell_draw(key_of[7], (FF, D), FF ** -0.5, 0.125, ((0, 4),)),
        "pre_attention": jnp.clip(jax.random.uniform(key_of[8], (D,), jnp.float32, -0.5, 0.5), -0.5, 0.5),
        "query_norm": jnp.clip(jax.random.uniform(key_of[9], (HEAD_DIM,), jnp.float32, -0.5, 0.5), -0.5, 0.5),
        "key_norm": jnp.clip(jax.random.uniform(key_of[10], (HEAD_DIM,), jnp.float32, -0.5, 0.5), -0.5, 0.5),
        "post_attention": jnp.clip(jax.random.uniform(key_of[11], (D,), jnp.float32, -0.5, 0.5), -0.5, 0.5),
        "pre_feedforward": jnp.clip(jax.random.uniform(key_of[12], (D,), jnp.float32, -0.5, 0.5), -0.5, 0.5),
        "post_feedforward": jnp.clip(jax.random.uniform(key_of[13], (D,), jnp.float32, -0.5, 0.5), -0.5, 0.5),
        "segments": draw_segments(jax.random.fold_in(key_of[17], 71), 0),
        "positions": draw_positions(jax.random.fold_in(key_of[17], 71), 0),
        "cotangent": bell_draw(key_of[16], (TOKENS, D), 1.0, 6.0, ((0, 8),)),
    }


@jax.custom_vjp
def low(v):
    return lax.optimization_barrier(v.astype(jnp.bfloat16)).astype(jnp.float32)

@jax.custom_vjp
def low_back(v):
    return v

def low_keep(v):
    return (low(v), None)

def low_pass(kept, grad):
    return (grad,)

def back_keep(v):
    return (v, None)

def back_low(kept, grad):
    return (low(grad),)
low.defvjp(low_keep, low_pass)
low_back.defvjp(back_keep, back_low)
epsilon = 1e-06
rope_base = 1000000.0
highest = lax.Precision.HIGHEST

def normed(values, norm_gain):
    inverse = lax.rsqrt(lax.optimization_barrier(jnp.mean(values * values, axis=-1, keepdims=True)) + epsilon)
    return values * inverse * (1.0 + norm_gain)

def rotary(values, cosine, sine_table):
    half_width = values.shape[-1] // 2
    front_half = values[..., :half_width]
    second = values[..., half_width:]
    return jnp.concatenate([front_half * cosine - second * sine_table, second * cosine + front_half * sine_table], axis=-1)

def rotary_tables(positions, head_width):
    steps_half = jnp.arange(head_width // 2).astype(jnp.float32)
    frequency = jnp.power(jnp.float32(rope_base), -2.0 * steps_half / head_width)
    angles = positions.astype(jnp.float32)[:, None] * frequency[None, :]
    return (jnp.cos(angles), jnp.sin(angles))

def layer(hidden, params, segments, positions):
    query_weight, key_weight, value_weight, output_weight, gate_weight, up_weight, down_weight, pre_attention, query_norm, key_norm, post_attention, pre_feedforward, post_feedforward = params
    tokens = hidden.shape[0]
    cosine, sine_table = rotary_tables(positions, HEAD_DIM)
    normed_in = low(normed(hidden, pre_attention))
    query_proj = low_back(jnp.dot(normed_in, query_weight, precision=highest)).reshape(tokens, HEADS, HEAD_DIM)
    key_proj = jnp.dot(normed_in, key_weight, precision=highest)
    value_low = low(jnp.dot(normed_in, value_weight, precision=highest))
    query_rot = low(rotary(normed(query_proj, query_norm), cosine[:, None, :], sine_table[:, None, :]))
    key_heads = low_back(jnp.broadcast_to(key_proj[None], (HEADS, tokens, HEAD_DIM)))
    key_rot = low(rotary(normed(key_heads, key_norm), cosine[None], sine_table[None]))
    value_heads = low_back(jnp.broadcast_to(value_low[None], (HEADS, tokens, HEAD_DIM)))
    scores = jnp.einsum('thd,hsd->hts', query_rot, key_rot, precision=highest) * HEAD_DIM ** (-0.5)
    scores = low_back(scores)
    offsets = jnp.arange(tokens)
    allowed = (segments[:, None] == segments[None, :]) & (offsets[None, :] <= offsets[:, None])
    scores = jnp.where(allowed[None], scores, -1e+30)
    top_score = lax.optimization_barrier(jnp.max(scores, axis=-1, keepdims=True))
    expo = jnp.exp(scores - top_score)
    prob_low = low(expo / lax.optimization_barrier(jnp.sum(expo, axis=-1, keepdims=True)))
    mixture = jnp.einsum('hts,hsd->thd', prob_low, value_heads, precision=highest).reshape(tokens, HEADS * HEAD_DIM)
    mixture = low_back(low(mixture))
    attention = low_back(jnp.dot(mixture, output_weight, precision=highest))
    middle = hidden + normed(attention, post_attention)
    normed_mid = low(normed(middle, pre_feedforward))
    gate_proj = low_back(jnp.dot(normed_mid, gate_weight, precision=highest))
    up_proj = low_back(jnp.dot(normed_mid, up_weight, precision=highest))
    product = low(jax.nn.gelu(gate_proj, approximate=True) * up_proj)
    feed = low_back(jnp.dot(product, down_weight, precision=highest))
    return middle + normed(feed, post_feedforward)

def reference(hidden_in, query_weight, key_weight, value_weight, output_weight, gate_weight, up_weight, down_weight, pre_attention, query_norm, key_norm, post_attention, pre_feedforward, post_feedforward, segments, positions, cotangent):
    params = (query_weight.astype(jnp.float32), key_weight.astype(jnp.float32), value_weight.astype(jnp.float32), output_weight.astype(jnp.float32), gate_weight.astype(jnp.float32), up_weight.astype(jnp.float32), down_weight.astype(jnp.float32), pre_attention.astype(jnp.float32), query_norm.astype(jnp.float32), key_norm.astype(jnp.float32), post_attention.astype(jnp.float32), pre_feedforward.astype(jnp.float32), post_feedforward.astype(jnp.float32))

    def one_pack(totals, block_index):
        first_row = (block_index * LEN).astype(jnp.int32)
        pack_rows = lax.dynamic_slice_in_dim(hidden_in, first_row, LEN, 0).astype(jnp.float32)
        pack_segments = lax.dynamic_slice_in_dim(segments, first_row, LEN, 0)
        pack_positions = lax.dynamic_slice_in_dim(positions, first_row, LEN, 0)
        pack_cotangent = lax.dynamic_slice_in_dim(cotangent, first_row, LEN, 0).astype(jnp.float32)

        def forward(rows_in, layer_params):
            return layer(rows_in, layer_params, pack_segments, pack_positions)
        layer_out, backward = jax.vjp(forward, pack_rows, params)
        grad_rows, grad_params = backward(pack_cotangent)
        totals = jax.tree.map(jnp.add, totals, grad_params)
        return (totals, (layer_out.astype(jnp.bfloat16), grad_rows))
    empty_grads = jax.tree.map(jnp.zeros_like, params)
    totals, (outputs, grad_inputs) = lax.scan(one_pack, empty_grads, jnp.arange(TOKENS // LEN, dtype=jnp.int32))
    return (outputs.reshape(TOKENS, D), grad_inputs.reshape(TOKENS, D), totals[0], totals[1], totals[2], totals[3], totals[4], totals[5], totals[6], totals[7], totals[8], totals[9], totals[10], totals[11], totals[12])
```

```python
import jax
import jax.numpy as jnp
from jax import lax
from jax.experimental import pallas as pl
from jax.experimental.pallas import tpu as pltpu
from jax.sharding import PartitionSpec as P

LEN = 512
EPS = 1e-06
ROPE_BASE = 1000000.0
MASKED = -1e30
LOW = jnp.bfloat16
F32 = jnp.float32
VMEM_LIMIT = 58 * 2**20


def dot(a, b, ca=1, cb=0):
    return lax.dot_general(a, b, (((ca,), (cb,)), ((), ())), preferred_element_type=F32)


def inverse_root(v):
    return lax.rsqrt(jnp.mean(v * v, axis=-1, keepdims=True) + EPS)


def norm_back(v, gain, c):
    r = inverse_root(v)
    n = v * r
    e = (1.0 + gain) * c
    return (
        r * (e - n * jnp.mean(e * n, axis=-1, keepdims=True)),
        jnp.sum(c * n, axis=0, keepdims=True),
    )


def rotate(u, cosine, sine):
    half = u.shape[-1] // 2
    a, b = u[:, :half], u[:, half:]
    return jnp.concatenate([a * cosine - b * sine, b * cosine + a * sine], axis=-1)


def rotate_back(w, cosine, sine):
    half = w.shape[-1] // 2
    a, b = w[:, :half], w[:, half:]
    return jnp.concatenate([a * cosine + b * sine, b * cosine - a * sine], axis=-1)


def call(body, outs, args, flops):
    return pl.pallas_call(
        body,
        out_shape=[jax.ShapeDtypeStruct(shape, kind) for shape, kind in outs],
        in_specs=[pl.BlockSpec(memory_space=pltpu.VMEM)] * len(args),
        out_specs=[pl.BlockSpec(memory_space=pltpu.VMEM)] * len(outs),
        compiler_params=pltpu.CompilerParams(vmem_limit_bytes=VMEM_LIMIT),
        cost_estimate=pl.CostEstimate(
            flops=flops,
            bytes_accessed=sum(a.size * a.dtype.itemsize for a in args),
            transcendentals=0,
        ),
    )(*args)


def attend_kernel(
    hidden, pre_attention, query_norm, key_norm, kw, vw, q0, q1, q2, q3, cosine, sine,
    seg_col, seg_row, normed_in, query_proj, key_proj, query_rot, key_rot, value_low,
    prob_low, mixture,
):
    h = hidden[...].astype(F32)
    x = (h * inverse_root(h) * (1.0 + pre_attention[...])).astype(LOW)
    normed_in[...] = x
    cos, sin = cosine[...], sine[...]
    k = dot(x, kw[...])
    key_proj[...] = k
    k = rotate(k * inverse_root(k) * (1.0 + key_norm[...]), cos, sin).astype(LOW)
    key_rot[...] = k
    v = dot(x, vw[...]).astype(LOW)
    value_low[...] = v
    scale = k.shape[-1] ** (-0.5)
    shape = (x.shape[0], x.shape[0])
    allowed = (seg_col[...] == seg_row[...]) & (
        lax.broadcasted_iota(jnp.int32, shape, 1) <= lax.broadcasted_iota(jnp.int32, shape, 0)
    )
    for r, qw in enumerate((q0, q1, q2, q3)):
        q = dot(x, qw[...])
        query_proj[r] = q
        q = rotate(q * inverse_root(q) * (1.0 + query_norm[...]), cos, sin).astype(LOW)
        query_rot[r] = q
        s = jnp.where(allowed, dot(q, k, 1, 1) * scale, MASKED)
        e = jnp.exp(s - jnp.max(s, axis=-1, keepdims=True))
        p = (e / jnp.sum(e, axis=-1, keepdims=True)).astype(LOW)
        prob_low[r] = p
        mixture[r] = dot(p, v).astype(LOW)


def middle_kernel(
    hidden, mixture, post_attention, pre_feedforward, o0, o1, o2, o3, attention, middle, normed_mid
):
    total = dot(mixture[0], o0[...])
    for r, ow in ((1, o1), (2, o2), (3, o3)):
        total = total + dot(mixture[r], ow[...])
    attention[...] = total
    m = hidden[...].astype(F32) + total * inverse_root(total) * (1.0 + post_attention[...])
    middle[...] = m
    normed_mid[...] = (m * inverse_root(m) * (1.0 + pre_feedforward[...])).astype(LOW)


GELU_A = 0.7978845608
GELU_B = 0.044715


def feed_kernel(
    attention, middle, normed_mid, cotangent, post_attention, pre_feedforward, post_feedforward,
    g0, g1, g2, g3, u0, u1, u2, u3, d0, d1, d2, d3,
    hidden_out, product_low, feed_grad_low, gate_grad_low, up_grad_low, middle_grad,
    attention_grad_low, grad_norms, gate_keep, up_keep,
):
    x = normed_mid[...]
    feed = None
    for r, (gw, uw, dw) in enumerate(((g0, u0, d0), (g1, u1, d1), (g2, u2, d2), (g3, u3, d3))):
        g = dot(x, gw[...])
        u = dot(x, uw[...])
        t = jnp.tanh(GELU_A * (g + GELU_B * (g * g * g)))
        act = 0.5 * g * (1.0 + t)
        slope = 0.5 * (1.0 + t) + 0.5 * g * (1.0 - t * t) * (
            GELU_A * (1.0 + 3.0 * GELU_B * g * g)
        )
        gate_keep[r] = u * slope
        up_keep[r] = act
        p = (act * u).astype(LOW)
        product_low[r] = p
        part = dot(p, dw[...])
        feed = part if feed is None else feed + part
    m = middle[...]
    hidden_out[...] = (m + feed * inverse_root(feed) * (1.0 + post_feedforward[...])).astype(LOW)
    c = cotangent[...].astype(F32)
    fg, grad_norms[0:1] = norm_back(feed, post_feedforward[...], c)
    fg = fg.astype(LOW)
    feed_grad_low[...] = fg
    total = None
    for r, (gw, uw, dw) in enumerate(((g0, u0, d0), (g1, u1, d1), (g2, u2, d2), (g3, u3, d3))):
        pg = dot(fg, dw[...], 1, 1)
        gg = (pg * gate_keep[r]).astype(LOW)
        ug = (pg * up_keep[r]).astype(LOW)
        gate_grad_low[r] = gg
        up_grad_low[r] = ug
        part = dot(gg, gw[...], 1, 1) + dot(ug, uw[...], 1, 1)
        total = part if total is None else total + part
    back, grad_norms[1:2] = norm_back(m, pre_feedforward[...], total)
    mg = c + back
    middle_grad[...] = mg
    ag, grad_norms[2:3] = norm_back(attention[...], post_attention[...], mg)
    attention_grad_low[...] = ag.astype(LOW)


def outer_units_kernel(a, b, keep, send):
    for r in range(4):
        out = (keep, send)[r % 2]
        out[r // 2] = dot(a[r], b[...], 0, 0).astype(LOW)


def outer_columns_kernel(a, b, keep, send):
    for r in range(4):
        out = (keep, send)[r % 2]
        out[r // 2] = dot(a[...], b[r], 0, 0).astype(LOW)


def attend_back_kernel(
    hidden, middle_grad, attention_grad_low, normed_in, query_proj, key_proj, query_rot, key_rot,
    value_low, prob_low, pre_attention, query_norm, key_norm, cosine, sine, kw, vw,
    q0, q1, q2, q3, o0, o1, o2, o3,
    grad_input, query_keep, query_send, grad_key, grad_value, grad_pre, grad_query_norm,
    grad_key_norm,
):
    cos, sin = cosine[...], sine[...]
    ag = attention_grad_low[...]
    x = normed_in[...]
    k = key_rot[...]
    v = value_low[...]
    scale = k.shape[-1] ** (-0.5)
    key_total = value_total = part = norm_total = None
    for r, (qw, ow) in enumerate(((q0, o0), (q1, o1), (q2, o2), (q3, o3))):
        mg = dot(ag, ow[...], 1, 1).astype(LOW)
        p = prob_low[r]
        pg = dot(mg, v, 1, 1)
        pf = p.astype(F32)
        s = (pf * (pg - jnp.sum(pf * pg, axis=-1, keepdims=True))).astype(LOW)
        qg = dot(s, k) * scale
        kg = dot(s, query_rot[r], 0, 0)
        vg = dot(p, mg, 0, 0)
        qg, gn = norm_back(query_proj[r], query_norm[...], rotate_back(qg, cos, sin))
        qg = qg.astype(LOW)
        out = (query_keep, query_send)[r % 2]
        out[r // 2] = dot(x, qg, 0, 0).astype(LOW)
        ip = dot(qg, qw[...], 1, 1)
        if r == 0:
            key_total, value_total, part, norm_total = kg, vg, ip, gn
        else:
            key_total = key_total + kg
            value_total = value_total + vg
            part = part + ip
            norm_total = norm_total + gn
    grad_query_norm[...] = norm_total
    kg, grad_key_norm[...] = norm_back(
        key_proj[...], key_norm[...], rotate_back(key_total * scale, cos, sin)
    )
    kg = kg.astype(LOW)
    vg = value_total.astype(LOW)
    grad_key[...] = dot(x, kg, 0, 0).astype(LOW)
    grad_value[...] = dot(x, vg, 0, 0).astype(LOW)
    part = part + dot(kg, kw[...], 1, 1) + dot(vg, vw[...], 1, 1)
    back, grad_pre[...] = norm_back(hidden[...].astype(F32), pre_attention[...], part)
    grad_input[...] = (middle_grad[...] + back).astype(LOW)


def swap(array, axis, count, bit):
    return lax.ppermute(array, axis, [(i, i ^ bit) for i in range(count)])


def add_low(a, b):
    return (a.astype(F32) + b.astype(F32)).astype(LOW)


def reduce_shards(keep, send, groups):
    merged = add_low(keep, swap(send, "tensor", 4, 1))
    own = add_low(merged[0], swap(merged[1], "tensor", 4, 2))
    me = lax.axis_index("dp")
    bits = []
    bit = 1
    while bit < groups:
        bits.append(bit)
        bit *= 2
    for bit in bits:
        high = (me // bit) % 2
        half = own.shape[0] // 2
        mine = lax.dynamic_slice_in_dim(own, high * half, half, 0)
        theirs = lax.dynamic_slice_in_dim(own, (1 - high) * half, half, 0)
        own = add_low(mine, swap(theirs, "dp", groups, bit))
    for bit in reversed(bits):
        high = (me // bit) % 2
        other = swap(own, "dp", groups, bit)
        own = jnp.where(
            high == 0,
            jnp.concatenate([own, other], axis=0),
            jnp.concatenate([other, own], axis=0),
        )
    return own


def on_device(groups):
    def run(
        hidden_in, query_weight, key_weight, value_weight, output_weight, gate_weight, up_weight,
        down_weight, pre_attention, query_norm, key_norm, post_attention, pre_feedforward,
        post_feedforward, segments, positions, cotangent,
    ):
        me = lax.axis_index("tensor")
        start = me * LEN
        width, head = key_weight.shape
        units = gate_weight.shape[1]

        def gathered(w):
            w2 = swap(w, "tensor", 4, 2)
            return [w, swap(w, "tensor", 4, 1), w2, swap(w2, "tensor", 4, 1)]

        queries = gathered(query_weight)
        outputs = gathered(output_weight)
        gates = gathered(gate_weight)
        ups = gathered(up_weight)
        downs = gathered(down_weight)

        hidden = lax.dynamic_slice_in_dim(hidden_in, start, LEN, 0)
        cot = lax.dynamic_slice_in_dim(cotangent, start, LEN, 0)
        segment = lax.dynamic_slice_in_dim(segments, start, LEN, 0)
        position = lax.dynamic_slice_in_dim(positions, start, LEN, 0)
        steps = jnp.arange(head // 2).astype(F32)
        frequency = jnp.power(F32(ROPE_BASE), -2.0 * steps / head)
        angles = position.astype(F32)[:, None] * frequency[None, :]
        cosine, sine = jnp.cos(angles), jnp.sin(angles)
        row = lambda v: v.reshape(1, -1)
        pre_a, pre_f = row(pre_attention), row(pre_feedforward)
        post_a, post_f = row(post_attention), row(post_feedforward)
        qn, kn = row(query_norm), row(key_norm)

        normed_in, query_proj, key_proj, query_rot, key_rot, value_low, prob_low, mixture = call(
            attend_kernel,
            [
                ((LEN, width), LOW), ((4, LEN, head), F32), ((LEN, head), F32),
                ((4, LEN, head), LOW), ((LEN, head), LOW), ((LEN, head), LOW),
                ((4, LEN, LEN), LOW), ((4, LEN, head), LOW),
            ],
            [
                hidden, pre_a, qn, kn, key_weight, value_weight, *queries, cosine, sine,
                segment[:, None], segment[None, :],
            ],
            4 * 10**9,
        )
        attention, middle, normed_mid = call(
            middle_kernel,
            [((LEN, width), F32), ((LEN, width), F32), ((LEN, width), LOW)],
            [hidden, mixture, post_a, pre_f, *outputs],
            10**9,
        )
        args = [attention, middle, normed_mid, cot, post_a, pre_f, post_f, *gates, *ups, *downs]
        outs = [
            ((LEN, width), LOW), ((4, LEN, units), LOW), ((LEN, width), LOW),
            ((4, LEN, units), LOW), ((4, LEN, units), LOW), ((LEN, width), F32),
            ((LEN, width), LOW), ((8, width), F32),
        ]
        (
            hidden_out, product_low, feed_grad_low, gate_grad_low, up_grad_low, middle_grad,
            attention_grad_low, grad_norms,
        ) = pl.pallas_call(
            feed_kernel,
            out_shape=[jax.ShapeDtypeStruct(shape, kind) for shape, kind in outs],
            in_specs=[pl.BlockSpec(memory_space=pltpu.VMEM)] * len(args),
            out_specs=[pl.BlockSpec(memory_space=pltpu.VMEM)] * len(outs),
            scratch_shapes=[pltpu.VMEM((4, LEN, units), F32)] * 2,
            compiler_params=pltpu.CompilerParams(vmem_limit_bytes=VMEM_LIMIT),
            cost_estimate=pl.CostEstimate(
                flops=10**10, bytes_accessed=2 * 10**7, transcendentals=0
            ),
        )(*args)
        hidden_out = lax.all_gather(hidden_out, "tensor", tiled=True)

        def outer(body, a, b, shape):
            return call(body, [((2, *shape), LOW)] * 2, [a, b], 14 * 10**8)

        down = outer(outer_units_kernel, product_low, feed_grad_low, (units, width))
        gate = outer(outer_columns_kernel, normed_mid, gate_grad_low, (width, units))
        up = outer(outer_columns_kernel, normed_mid, up_grad_low, (width, units))
        output = outer(outer_units_kernel, mixture, attention_grad_low, (head, width))
        (
            grad_input, query_keep, query_send, grad_key, grad_value, grad_pre, grad_qn, grad_kn,
        ) = call(
            attend_back_kernel,
            [
                ((LEN, width), LOW), ((2, width, head), LOW), ((2, width, head), LOW),
                ((width, head), LOW), ((width, head), LOW), ((1, width), F32), ((1, head), F32),
                ((1, head), F32),
            ],
            [
                hidden, middle_grad, attention_grad_low, normed_in, query_proj, key_proj,
                query_rot, key_rot, value_low, prob_low, pre_a, qn, kn, cosine, sine, key_weight,
                value_weight, *queries, *outputs,
            ],
            6 * 10**9,
        )
        grad_input = lax.all_gather(grad_input, "tensor", tiled=True).astype(F32)

        small = jnp.concatenate(
            [grad_norms[:3].reshape(-1), grad_pre[0], grad_qn[0], grad_kn[0]]
        ).astype(LOW)
        quarter = (2 * width + 256) // 4
        small = jnp.pad(small, (0, 256 * head - small.shape[0])).reshape(256, head)
        shared = jnp.concatenate([grad_key, grad_value, small], axis=0)
        parts = [
            lax.dynamic_slice_in_dim(shared, (me ^ r) * quarter, quarter, 0) for r in range(4)
        ]
        keep = jnp.concatenate([query_keep, jnp.stack([parts[0], parts[2]])], axis=1)
        send = jnp.concatenate([query_send, jnp.stack([parts[1], parts[3]])], axis=1)

        grad_down = reduce_shards(*down, groups).astype(F32)
        grad_gate = reduce_shards(*gate, groups).astype(F32)
        grad_up = reduce_shards(*up, groups).astype(F32)
        grad_output = reduce_shards(*output, groups).astype(F32)
        last = reduce_shards(keep, send, groups)
        grad_query = last[:width].astype(F32)
        shared = lax.all_gather(last[width:], "tensor", tiled=True).astype(F32)
        small = shared[2 * width :].reshape(-1)
        cuts = [0]
        for size in (width, width, width, width, head, head):
            cuts.append(cuts[-1] + size)
        post_f, pre_f, post_a, pre_a, qn, kn = [
            small[a:b] for a, b in zip(cuts[:-1], cuts[1:])
        ]
        return (
            hidden_out, grad_input, grad_query, shared[:width], shared[width : 2 * width],
            grad_output, grad_gate, grad_up, grad_down, pre_a, qn, kn, post_a, pre_f, post_f,
        )

    return run


def solution(mesh):
    placed = (
        P("dp", None), P(None, "tensor"), P(), P(), P("tensor", None), P(None, "tensor"),
        P(None, "tensor"), P("tensor", None), P(), P(), P(), P(), P(), P(), P("dp"), P("dp"),
        P("dp", None),
    )
    return jax.shard_map(
        on_device(mesh.shape["dp"]),
        mesh=mesh,
        in_specs=placed,
        out_specs=(
            P("dp", None), P("dp", None), P(None, "tensor"), P(), P(), P("tensor", None),
            P(None, "tensor"), P(None, "tensor"), P("tensor", None), P(), P(), P(), P(), P(), P(),
        ),
        check_vma=False,
    )
```

```python
import jax
import jax.numpy as jnp
from jax import lax
from jax.experimental import pallas as pl
from jax.experimental.pallas import tpu as pltpu
from jax.sharding import PartitionSpec as P

LEN = 512
EPS = 1e-06
ROPE_BASE = 1000000.0
MASKED = -1e30
LOW = jnp.bfloat16
F32 = jnp.float32
VMEM_LIMIT = 58 * 2**20


def dot(a, b, ca=1, cb=0):
    return lax.dot_general(a, b, (((ca,), (cb,)), ((), ())), preferred_element_type=F32)


def inverse_root(v):
    return lax.rsqrt(jnp.mean(v * v, axis=-1, keepdims=True) + EPS)


def norm_back(v, gain, c):
    r = inverse_root(v)
    n = v * r
    e = (1.0 + gain) * c
    return (
        r * (e - n * jnp.mean(e * n, axis=-1, keepdims=True)),
        jnp.sum(c * n, axis=0, keepdims=True),
    )


def rotate(u, cosine, sine):
    half = u.shape[-1] // 2
    a, b = u[:, :half], u[:, half:]
    return jnp.concatenate([a * cosine - b * sine, b * cosine + a * sine], axis=-1)


def rotate_back(w, cosine, sine):
    half = w.shape[-1] // 2
    a, b = w[:, :half], w[:, half:]
    return jnp.concatenate([a * cosine + b * sine, b * cosine - a * sine], axis=-1)


def call(body, outs, args, flops):
    return pl.pallas_call(
        body,
        out_shape=[jax.ShapeDtypeStruct(shape, kind) for shape, kind in outs],
        in_specs=[pl.BlockSpec(memory_space=pltpu.VMEM)] * len(args),
        out_specs=[pl.BlockSpec(memory_space=pltpu.VMEM)] * len(outs),
        compiler_params=pltpu.CompilerParams(vmem_limit_bytes=VMEM_LIMIT),
        cost_estimate=pl.CostEstimate(
            flops=flops,
            bytes_accessed=sum(a.size * a.dtype.itemsize for a in args),
            transcendentals=0,
        ),
    )(*args)


def attend_kernel(
    hidden, pre_attention, query_norm, key_norm, kw, vw, q0, q1, q2, q3, cosine, sine,
    seg_col, seg_row, normed_in, query_proj, key_proj, query_rot, key_rot, value_low,
    prob_low, mixture,
):
    h = hidden[...].astype(F32)
    x = (h * inverse_root(h) * (1.0 + pre_attention[...])).astype(LOW)
    normed_in[...] = x
    cos, sin = cosine[...], sine[...]
    k = dot(x, kw[...])
    key_proj[...] = k
    k = rotate(k * inverse_root(k) * (1.0 + key_norm[...]), cos, sin).astype(LOW)
    key_rot[...] = k
    v = dot(x, vw[...]).astype(LOW)
    value_low[...] = v
    scale = k.shape[-1] ** (-0.5)
    shape = (x.shape[0], x.shape[0])
    allowed = (seg_col[...] == seg_row[...]) & (
        lax.broadcasted_iota(jnp.int32, shape, 1) <= lax.broadcasted_iota(jnp.int32, shape, 0)
    )
    for r, qw in enumerate((q0, q1, q2, q3)):
        q = dot(x, qw[...])
        query_proj[r] = q
        q = rotate(q * inverse_root(q) * (1.0 + query_norm[...]), cos, sin).astype(LOW)
        query_rot[r] = q
        s = jnp.where(allowed, dot(q, k, 1, 1) * scale, MASKED)
        e = jnp.exp(s - jnp.max(s, axis=-1, keepdims=True))
        p = (e / jnp.sum(e, axis=-1, keepdims=True)).astype(LOW)
        prob_low[r] = p
        mixture[r] = dot(p, v).astype(LOW)


def middle_kernel(
    hidden, mixture, post_attention, pre_feedforward, o0, o1, o2, o3, attention, middle, normed_mid
):
    total = dot(mixture[0], o0[...])
    for r, ow in ((1, o1), (2, o2), (3, o3)):
        total = total + dot(mixture[r], ow[...])
    attention[...] = total
    m = hidden[...].astype(F32) + total * inverse_root(total) * (1.0 + post_attention[...])
    middle[...] = m
    normed_mid[...] = (m * inverse_root(m) * (1.0 + pre_feedforward[...])).astype(LOW)


GELU_A = 0.7978845608
GELU_B = 0.044715


def feed_kernel(
    attention, middle, normed_mid, cotangent, post_attention, pre_feedforward, post_feedforward,
    g0, g1, g2, g3, u0, u1, u2, u3, d0, d1, d2, d3,
    hidden_out, product_low, feed_grad_low, gate_grad_low, up_grad_low, middle_grad,
    attention_grad_low, grad_norms, gate_keep, up_keep,
):
    x = normed_mid[...]
    feed = None
    for r, (gw, uw, dw) in enumerate(((g0, u0, d0), (g1, u1, d1), (g2, u2, d2), (g3, u3, d3))):
        g = dot(x, gw[...])
        u = dot(x, uw[...])
        t = jnp.tanh(GELU_A * (g + GELU_B * (g * g * g)))
        act = 0.5 * g * (1.0 + t)
        slope = 0.5 * (1.0 + t) + 0.5 * g * (1.0 - t * t) * (
            GELU_A * (1.0 + 3.0 * GELU_B * g * g)
        )
        gate_keep[r] = u * slope
        up_keep[r] = act
        p = (act * u).astype(LOW)
        product_low[r] = p
        part = dot(p, dw[...])
        feed = part if feed is None else feed + part
    m = middle[...]
    hidden_out[...] = (m + feed * inverse_root(feed) * (1.0 + post_feedforward[...])).astype(LOW)
    c = cotangent[...].astype(F32)
    fg, grad_norms[0:1] = norm_back(feed, post_feedforward[...], c)
    fg = fg.astype(LOW)
    feed_grad_low[...] = fg
    total = None
    for r, (gw, uw, dw) in enumerate(((g0, u0, d0), (g1, u1, d1), (g2, u2, d2), (g3, u3, d3))):
        pg = dot(fg, dw[...], 1, 1)
        gg = (pg * gate_keep[r]).astype(LOW)
        ug = (pg * up_keep[r]).astype(LOW)
        gate_grad_low[r] = gg
        up_grad_low[r] = ug
        part = dot(gg, gw[...], 1, 1) + dot(ug, uw[...], 1, 1)
        total = part if total is None else total + part
    back, grad_norms[1:2] = norm_back(m, pre_feedforward[...], total)
    mg = c + back
    middle_grad[...] = mg
    ag, grad_norms[2:3] = norm_back(attention[...], post_attention[...], mg)
    attention_grad_low[...] = ag.astype(LOW)


def outer_units_kernel(a, b, keep, send):
    for r in range(4):
        out = (keep, send)[r % 2]
        out[r // 2] = dot(a[r], b[...], 0, 0).astype(LOW)


def outer_columns_kernel(a, b, keep, send):
    for r in range(4):
        out = (keep, send)[r % 2]
        out[r // 2] = dot(a[...], b[r], 0, 0).astype(LOW)


def attend_back_kernel(
    hidden, middle_grad, attention_grad_low, normed_in, query_proj, key_proj, query_rot, key_rot,
    value_low, prob_low, pre_attention, query_norm, key_norm, cosine, sine, kw, vw,
    q0, q1, q2, q3, o0, o1, o2, o3,
    grad_input, query_keep, query_send, grad_key, grad_value, grad_pre, grad_query_norm,
    grad_key_norm,
):
    cos, sin = cosine[...], sine[...]
    ag = attention_grad_low[...]
    x = normed_in[...]
    k = key_rot[...]
    v = value_low[...]
    scale = k.shape[-1] ** (-0.5)
    key_total = value_total = part = norm_total = None
    for r, (qw, ow) in enumerate(((q0, o0), (q1, o1), (q2, o2), (q3, o3))):
        mg = dot(ag, ow[...], 1, 1).astype(LOW)
        p = prob_low[r]
        pg = dot(mg, v, 1, 1)
        pf = p.astype(F32)
        s = (pf * (pg - jnp.sum(pf * pg, axis=-1, keepdims=True))).astype(LOW)
        qg = dot(s, k) * scale
        kg = dot(s, query_rot[r], 0, 0)
        vg = dot(p, mg, 0, 0)
        qg, gn = norm_back(query_proj[r], query_norm[...], rotate_back(qg, cos, sin))
        qg = qg.astype(LOW)
        out = (query_keep, query_send)[r % 2]
        out[r // 2] = dot(x, qg, 0, 0).astype(LOW)
        ip = dot(qg, qw[...], 1, 1)
        if r == 0:
            key_total, value_total, part, norm_total = kg, vg, ip, gn
        else:
            key_total = key_total + kg
            value_total = value_total + vg
            part = part + ip
            norm_total = norm_total + gn
    grad_query_norm[...] = norm_total
    kg, grad_key_norm[...] = norm_back(
        key_proj[...], key_norm[...], rotate_back(key_total * scale, cos, sin)
    )
    kg = kg.astype(LOW)
    vg = value_total.astype(LOW)
    grad_key[...] = dot(x, kg, 0, 0).astype(LOW)
    grad_value[...] = dot(x, vg, 0, 0).astype(LOW)
    part = part + dot(kg, kw[...], 1, 1) + dot(vg, vw[...], 1, 1)
    back, grad_pre[...] = norm_back(hidden[...].astype(F32), pre_attention[...], part)
    grad_input[...] = (middle_grad[...] + back).astype(LOW)


def swap(array, axis, count, bit):
    return lax.ppermute(array, axis, [(i, i ^ bit) for i in range(count)])


def add_low(a, b):
    return (a.astype(F32) + b.astype(F32)).astype(LOW)


CHUNKS = 5
QUARTER = 384


def plan_steps(groups, rows):
    steps = []
    bit = 1
    while bit < groups:
        halved = rows % 32 == 0
        rows = rows // 2 if halved else rows
        steps.append((bit, halved, rows))
        bit *= 2
    return steps


def reduce_kernel(groups, shapes, *refs):
    refs = list(refs)
    take = lambda n: [refs.pop(0) for _ in range(n)]
    pairs = take(2 * CHUNKS)
    (grad_input,) = take(1)
    outs = take(CHUNKS)
    shared_out, input_out = take(2)
    from_core = take(CHUNKS)
    merged = take(CHUNKS)
    from_second = take(CHUNKS)
    plans = [plan_steps(groups, rows) for rows, _ in shapes]
    halves = [take(len(p)) for p in plans]
    sums = [take(len(p) + 1) for p in plans]
    full = take(CHUNKS)
    shared, inputs, send_sem, recv_sem = take(4)
    me = lax.axis_index("tensor")
    group = lax.axis_index("dp")
    bits = [p[0] for p in plans[0]]
    targets = [{"tensor": me ^ 1}, {"tensor": me ^ 2}] + [{"dp": group ^ bit} for bit in bits]
    barrier = pltpu.get_barrier_semaphore()
    for target in targets:
        pl.semaphore_signal(
            barrier, inc=1, device_id=target, device_id_type=pl.DeviceIdType.MESH
        )
    pl.semaphore_wait(barrier, len(targets))
    started = []

    def send(source, landing, target):
        slot = len(started)
        copy = pltpu.make_async_remote_copy(
            src_ref=source,
            dst_ref=landing,
            send_sem=send_sem.at[slot],
            recv_sem=recv_sem.at[slot],
            device_id=target,
            device_id_type=pl.DeviceIdType.MESH,
        )
        copy.start()
        started.append(copy)
        return copy

    core, second = targets[:2]

    def chunk(c, first):
        rows, columns = shapes[c]
        size = rows * columns / 5e4
        plan = plans[c]
        keep = pairs[2 * c]
        offset = 0
        own = sums[c]
        first.wait_recv()
        merged[c][1] = add_low(keep[1], from_core[c][1])
        copy = send(merged[c].at[1], from_second[c], second)
        merged[c][0] = add_low(keep[0], from_core[c][0])
        yield 0.0
        copy.wait_recv()
        own[0][...] = add_low(merged[c][0], from_second[c][...])
        for i, (bit, halved, count) in enumerate(plan):
            high = (group // bit) % 2
            target = {"dp": group ^ bit}
            if halved:
                mine = pl.ds(pl.multiple_of(high * count, 16), count)
                theirs = pl.ds(pl.multiple_of((1 - high) * count, 16), count)
                offset = offset + high * count
            else:
                mine = theirs = pl.ds(0, count)
            copy = send(own[i].at[theirs], halves[c][i], target)
            yield size * count / rows + 2.0
            copy.wait_recv()
            own[i + 1][...] = add_low(own[i][mine], halves[c][i][...])
        count = plan[-1][2]
        full[c][pl.ds(pl.multiple_of(offset, 16), count)] = own[-1][...]
        for bit, halved, count in reversed(plan):
            if not halved:
                continue
            piece = pl.ds(pl.multiple_of(offset, 16), count)
            copy = send(full[c].at[piece], full[c].at[piece], {"dp": group ^ bit})
            yield size * count / rows + 2.0
            copy.wait_recv()
            offset = offset - (group // bit) % 2 * count
        outs[c][...] = full[c][...]
        if c == CHUNKS - 1:
            shared[me] = full[c][rows - QUARTER :]
            one = send(shared.at[me], shared.at[me], second)
            two = send(shared.at[me], shared.at[me], core)
            yield 4.0
            one.wait_recv()
            three = send(shared.at[me ^ 2], shared.at[me ^ 2], core)
            yield 2.0
            two.wait_recv()
            three.wait_recv()
            for r in range(4):
                shared_out[r] = shared[r]

    firsts = [send(pairs[2 * c + 1], from_core[c], core) for c in range(CHUNKS)]
    work = [chunk(c, firsts[c]) for c in range(CHUNKS)]
    ready = 3.0
    due = []
    for c in range(CHUNKS):
        next(work[c])
        ready += shapes[c][0] * shapes[c][1] / 2.4e4
        due.append(ready)
        if c == 2:
            inputs[me] = grad_input[...]
    one = send(inputs.at[me], inputs.at[me], second)
    two = send(inputs.at[me], inputs.at[me], core)
    input_due = ready + 14.0
    three = None
    live = set(range(CHUNKS))
    while live or three is None:
        if three is None and (not live or input_due < min(due[c] for c in live)):
            one.wait_recv()
            three = send(inputs.at[me ^ 2], inputs.at[me ^ 2], core)
            continue
        c = min(live, key=lambda i: (due[i], i))
        step = next(work[c], None)
        if step is None:
            live.remove(c)
        else:
            due[c] += step
    two.wait_recv()
    three.wait_recv()
    for r in range(4):
        input_out[r] = inputs[r]
    for copy in started:
        copy.wait_send()


def reduce_all(groups, pairs, grad_input):
    shapes = [keep.shape[1:] for keep, _ in pairs]
    plans = [plan_steps(groups, rows) for rows, _ in shapes]
    args = [a for pair in pairs for a in pair] + [grad_input]
    low = lambda *shape: pltpu.VMEM(shape, LOW)
    outs = [jax.ShapeDtypeStruct(shape, LOW) for shape in shapes]
    outs.append(jax.ShapeDtypeStruct((4, QUARTER, shapes[-1][1]), LOW))
    outs.append(jax.ShapeDtypeStruct((4, *grad_input.shape), LOW))
    scratch = [low(2, *shape) for shape in shapes] * 2 + [low(*shape) for shape in shapes]
    for plan, (_, columns) in zip(plans, shapes):
        scratch += [low(count, columns) for _, _, count in plan]
    for plan, (rows, columns) in zip(plans, shapes):
        scratch += [low(rows, columns)] + [low(count, columns) for _, _, count in plan]
    scratch += [low(*shape) for shape in shapes]
    scratch += [low(*outs[-2].shape), low(*outs[-1].shape)]
    copies = 2 * CHUNKS + 6 + sum(1 + halved for plan in plans for _, halved, _ in plan)
    scratch += [pltpu.SemaphoreType.DMA((copies,))] * 2

    def body(*refs):
        reduce_kernel(groups, shapes, *refs)

    return pl.pallas_call(
        body,
        out_shape=outs,
        in_specs=[pl.BlockSpec(memory_space=pltpu.VMEM)] * len(args),
        out_specs=[pl.BlockSpec(memory_space=pltpu.VMEM)] * len(outs),
        scratch_shapes=scratch,
        compiler_params=pltpu.CompilerParams(
            vmem_limit_bytes=VMEM_LIMIT, collective_id=0, has_side_effects=True
        ),
        cost_estimate=pl.CostEstimate(flops=10**7, bytes_accessed=10**8, transcendentals=0),
    )(*args)


def on_device(groups):
    def run(
        hidden_in, query_weight, key_weight, value_weight, output_weight, gate_weight, up_weight,
        down_weight, pre_attention, query_norm, key_norm, post_attention, pre_feedforward,
        post_feedforward, segments, positions, cotangent,
    ):
        me = lax.axis_index("tensor")
        start = me * LEN
        width, head = key_weight.shape
        units = gate_weight.shape[1]

        shards = [query_weight, output_weight, gate_weight, up_weight, down_weight]
        seconds = [swap(w, "tensor", 4, 2) for w in shards]

        def gathered(i, second):
            w = shards[i]
            return [w, swap(w, "tensor", 4, 1), second, swap(second, "tensor", 4, 1)]

        queries = gathered(0, seconds[0])

        hidden = lax.dynamic_slice_in_dim(hidden_in, start, LEN, 0)
        cot = lax.dynamic_slice_in_dim(cotangent, start, LEN, 0)
        segment = lax.dynamic_slice_in_dim(segments, start, LEN, 0)
        position = lax.dynamic_slice_in_dim(positions, start, LEN, 0)
        steps = jnp.arange(head // 2).astype(F32)
        frequency = jnp.power(F32(ROPE_BASE), -2.0 * steps / head)
        angles = position.astype(F32)[:, None] * frequency[None, :]
        cosine, sine = jnp.cos(angles), jnp.sin(angles)
        row = lambda v: v.reshape(1, -1)
        pre_a, pre_f = row(pre_attention), row(pre_feedforward)
        post_a, post_f = row(post_attention), row(post_feedforward)
        qn, kn = row(query_norm), row(key_norm)

        normed_in, query_proj, key_proj, query_rot, key_rot, value_low, prob_low, mixture = call(
            attend_kernel,
            [
                ((LEN, width), LOW), ((4, LEN, head), F32), ((LEN, head), F32),
                ((4, LEN, head), LOW), ((LEN, head), LOW), ((LEN, head), LOW),
                ((4, LEN, LEN), LOW), ((4, LEN, head), LOW),
            ],
            [
                hidden, pre_a, qn, kn, key_weight, value_weight, *queries, cosine, sine,
                segment[:, None], segment[None, :],
            ],
            4 * 10**9,
        )
        mixture, *seconds = lax.optimization_barrier((mixture, *seconds[1:]))
        outputs = gathered(1, seconds[0])
        attention, middle, normed_mid = call(
            middle_kernel,
            [((LEN, width), F32), ((LEN, width), F32), ((LEN, width), LOW)],
            [hidden, mixture, post_a, pre_f, *outputs],
            10**9,
        )
        normed_mid, *seconds = lax.optimization_barrier((normed_mid, *seconds[1:]))
        gates, ups, downs = [gathered(i + 2, seconds[i]) for i in range(3)]
        args = [attention, middle, normed_mid, cot, post_a, pre_f, post_f, *gates, *ups, *downs]
        outs = [
            ((LEN, width), LOW), ((4, LEN, units), LOW), ((LEN, width), LOW),
            ((4, LEN, units), LOW), ((4, LEN, units), LOW), ((LEN, width), F32),
            ((LEN, width), LOW), ((8, width), F32),
        ]
        (
            hidden_out, product_low, feed_grad_low, gate_grad_low, up_grad_low, middle_grad,
            attention_grad_low, grad_norms,
        ) = pl.pallas_call(
            feed_kernel,
            out_shape=[jax.ShapeDtypeStruct(shape, kind) for shape, kind in outs],
            in_specs=[pl.BlockSpec(memory_space=pltpu.VMEM)] * len(args),
            out_specs=[pl.BlockSpec(memory_space=pltpu.VMEM)] * len(outs),
            scratch_shapes=[pltpu.VMEM((4, LEN, units), F32)] * 2,
            compiler_params=pltpu.CompilerParams(vmem_limit_bytes=VMEM_LIMIT),
            cost_estimate=pl.CostEstimate(
                flops=10**10, bytes_accessed=2 * 10**7, transcendentals=0
            ),
        )(*args)
        hidden_out = lax.all_gather(hidden_out, "tensor", tiled=True)

        def outer(body, a, b, shape):
            return call(body, [((2, *shape), LOW)] * 2, [a, b], 14 * 10**8)

        down = outer(outer_units_kernel, product_low, feed_grad_low, (units, width))
        gate = outer(outer_columns_kernel, normed_mid, gate_grad_low, (width, units))
        up = outer(outer_columns_kernel, normed_mid, up_grad_low, (width, units))
        output = outer(outer_units_kernel, mixture, attention_grad_low, (head, width))
        (
            grad_input, query_keep, query_send, grad_key, grad_value, grad_pre, grad_qn, grad_kn,
        ) = call(
            attend_back_kernel,
            [
                ((LEN, width), LOW), ((2, width, head), LOW), ((2, width, head), LOW),
                ((width, head), LOW), ((width, head), LOW), ((1, width), F32), ((1, head), F32),
                ((1, head), F32),
            ],
            [
                hidden, middle_grad, attention_grad_low, normed_in, query_proj, key_proj,
                query_rot, key_rot, value_low, prob_low, pre_a, qn, kn, cosine, sine, key_weight,
                value_weight, *queries, *outputs,
            ],
            6 * 10**9,
        )
        small = jnp.concatenate(
            [grad_norms[:3].reshape(-1), grad_pre[0], grad_qn[0], grad_kn[0]]
        ).astype(LOW)
        quarter = QUARTER
        small = jnp.pad(small, (0, 256 * head - small.shape[0])).reshape(256, head)
        shared = jnp.concatenate([grad_key, grad_value, small], axis=0)
        parts = [
            lax.dynamic_slice_in_dim(shared, (me ^ r) * quarter, quarter, 0) for r in range(4)
        ]
        keep = jnp.concatenate([query_keep, jnp.stack([parts[0], parts[2]])], axis=1)
        send = jnp.concatenate([query_send, jnp.stack([parts[1], parts[3]])], axis=1)

        *grads, shared, grad_input = reduce_all(
            groups, [down, gate, up, output, (keep, send)], grad_input
        )
        grad_down, grad_gate, grad_up, grad_output = [g.astype(F32) for g in grads[:4]]
        grad_query = grads[4][:width].astype(F32)
        shared = shared.reshape(-1, head).astype(F32)
        grad_input = grad_input.reshape(-1, width).astype(F32)
        small = shared[2 * width :].reshape(-1)
        cuts = [0]
        for size in (width, width, width, width, head, head):
            cuts.append(cuts[-1] + size)
        post_f, pre_f, post_a, pre_a, qn, kn = [
            small[a:b] for a, b in zip(cuts[:-1], cuts[1:])
        ]
        return (
            hidden_out, grad_input, grad_query, shared[:width], shared[width : 2 * width],
            grad_output, grad_gate, grad_up, grad_down, pre_a, qn, kn, post_a, pre_f, post_f,
        )

    return run


def solution(mesh):
    placed = (
        P("dp", None), P(None, "tensor"), P(), P(), P("tensor", None), P(None, "tensor"),
        P(None, "tensor"), P("tensor", None), P(), P(), P(), P(), P(), P(), P("dp"), P("dp"),
        P("dp", None),
    )
    return jax.shard_map(
        on_device(mesh.shape["dp"]),
        mesh=mesh,
        in_specs=placed,
        out_specs=(
            P("dp", None), P("dp", None), P(None, "tensor"), P(), P(), P("tensor", None),
            P(None, "tensor"), P(None, "tensor"), P("tensor", None), P(), P(), P(), P(), P(), P(),
        ),
        check_vma=False,
    )
```

```python
import jax
import jax.numpy as jnp
from jax import lax
from jax.experimental import pallas as pl
from jax.experimental.pallas import tpu as pltpu
from jax.sharding import PartitionSpec as P

LEN = 512
EPS = 1e-06
ROPE_BASE = 1000000.0
MASKED = -1e30
LOW = jnp.bfloat16
F32 = jnp.float32
VMEM_LIMIT = 58 * 2**20


def dot(a, b, ca=1, cb=0):
    return lax.dot_general(a, b, (((ca,), (cb,)), ((), ())), preferred_element_type=F32)


def inverse_root(v):
    return lax.rsqrt(jnp.mean(v * v, axis=-1, keepdims=True) + EPS)


def norm_back(v, gain, c):
    r = inverse_root(v)
    n = v * r
    e = (1.0 + gain) * c
    return (
        r * (e - n * jnp.mean(e * n, axis=-1, keepdims=True)),
        jnp.sum(c * n, axis=0, keepdims=True),
    )


def rotate(u, cosine, sine):
    half = u.shape[-1] // 2
    a, b = u[:, :half], u[:, half:]
    return jnp.concatenate([a * cosine - b * sine, b * cosine + a * sine], axis=-1)


def rotate_back(w, cosine, sine):
    half = w.shape[-1] // 2
    a, b = w[:, :half], w[:, half:]
    return jnp.concatenate([a * cosine + b * sine, b * cosine - a * sine], axis=-1)


def call(body, outs, args, flops):
    return pl.pallas_call(
        body,
        out_shape=[jax.ShapeDtypeStruct(shape, kind) for shape, kind in outs],
        in_specs=[pl.BlockSpec(memory_space=pltpu.VMEM)] * len(args),
        out_specs=[pl.BlockSpec(memory_space=pltpu.VMEM)] * len(outs),
        compiler_params=pltpu.CompilerParams(vmem_limit_bytes=VMEM_LIMIT),
        cost_estimate=pl.CostEstimate(
            flops=flops,
            bytes_accessed=sum(a.size * a.dtype.itemsize for a in args),
            transcendentals=0,
        ),
    )(*args)


def attend_kernel(
    hidden, pre_attention, query_norm, key_norm, kw, vw, q0, q1, q2, q3, cosine, sine,
    seg_col, seg_row, normed_in, query_proj, key_proj, query_rot, key_rot, value_low,
    prob_low, mixture,
):
    h = hidden[...].astype(F32)
    x = (h * inverse_root(h) * (1.0 + pre_attention[...])).astype(LOW)
    normed_in[...] = x
    cos, sin = cosine[...], sine[...]
    k = dot(x, kw[...])
    key_proj[...] = k
    k = rotate(k * inverse_root(k) * (1.0 + key_norm[...]), cos, sin).astype(LOW)
    key_rot[...] = k
    v = dot(x, vw[...]).astype(LOW)
    value_low[...] = v
    scale = k.shape[-1] ** (-0.5)
    shape = (x.shape[0], x.shape[0])
    allowed = (seg_col[...] == seg_row[...]) & (
        lax.broadcasted_iota(jnp.int32, shape, 1) <= lax.broadcasted_iota(jnp.int32, shape, 0)
    )
    for r, qw in enumerate((q0, q1, q2, q3)):
        q = dot(x, qw[...])
        query_proj[r] = q
        q = rotate(q * inverse_root(q) * (1.0 + query_norm[...]), cos, sin).astype(LOW)
        query_rot[r] = q
        s = jnp.where(allowed, dot(q, k, 1, 1) * scale, MASKED)
        e = jnp.exp(s - jnp.max(s, axis=-1, keepdims=True))
        p = (e / jnp.sum(e, axis=-1, keepdims=True)).astype(LOW)
        prob_low[r] = p
        mixture[r] = dot(p, v).astype(LOW)


def middle_kernel(
    hidden, mixture, post_attention, pre_feedforward, o0, o1, o2, o3, attention, middle, normed_mid
):
    total = dot(mixture[0], o0[...])
    for r, ow in ((1, o1), (2, o2), (3, o3)):
        total = total + dot(mixture[r], ow[...])
    attention[...] = total
    m = hidden[...].astype(F32) + total * inverse_root(total) * (1.0 + post_attention[...])
    middle[...] = m
    normed_mid[...] = (m * inverse_root(m) * (1.0 + pre_feedforward[...])).astype(LOW)


GELU_A = 0.7978845608
GELU_B = 0.044715


def feed_kernel(
    attention, middle, normed_mid, cotangent, post_attention, pre_feedforward, post_feedforward,
    g0, g1, g2, g3, u0, u1, u2, u3, d0, d1, d2, d3,
    hidden_out, product_low, feed_grad_low, gate_grad_low, up_grad_low, middle_grad,
    attention_grad_low, grad_norms, gate_keep, up_keep,
):
    x = normed_mid[...]
    feed = None
    for r, (gw, uw, dw) in enumerate(((g0, u0, d0), (g1, u1, d1), (g2, u2, d2), (g3, u3, d3))):
        g = dot(x, gw[...])
        u = dot(x, uw[...])
        t = jnp.tanh(GELU_A * (g + GELU_B * (g * g * g)))
        act = 0.5 * g * (1.0 + t)
        slope = 0.5 * (1.0 + t) + 0.5 * g * (1.0 - t * t) * (
            GELU_A * (1.0 + 3.0 * GELU_B * g * g)
        )
        gate_keep[r] = u * slope
        up_keep[r] = act
        p = (act * u).astype(LOW)
        product_low[r] = p
        part = dot(p, dw[...])
        feed = part if feed is None else feed + part
    m = middle[...]
    hidden_out[...] = (m + feed * inverse_root(feed) * (1.0 + post_feedforward[...])).astype(LOW)
    c = cotangent[...].astype(F32)
    fg, grad_norms[0:1] = norm_back(feed, post_feedforward[...], c)
    fg = fg.astype(LOW)
    feed_grad_low[...] = fg
    total = None
    for r, (gw, uw, dw) in enumerate(((g0, u0, d0), (g1, u1, d1), (g2, u2, d2), (g3, u3, d3))):
        pg = dot(fg, dw[...], 1, 1)
        gg = (pg * gate_keep[r]).astype(LOW)
        ug = (pg * up_keep[r]).astype(LOW)
        gate_grad_low[r] = gg
        up_grad_low[r] = ug
        part = dot(gg, gw[...], 1, 1) + dot(ug, uw[...], 1, 1)
        total = part if total is None else total + part
    back, grad_norms[1:2] = norm_back(m, pre_feedforward[...], total)
    mg = c + back
    middle_grad[...] = mg
    ag, grad_norms[2:3] = norm_back(attention[...], post_attention[...], mg)
    attention_grad_low[...] = ag.astype(LOW)


def outer_units_kernel(a, b, keep, send):
    for r in range(4):
        out = (keep, send)[r % 2]
        out[r // 2] = dot(a[r], b[...], 0, 0).astype(LOW)


def outer_columns_kernel(a, b, keep, send):
    for r in range(4):
        out = (keep, send)[r % 2]
        out[r // 2] = dot(a[...], b[r], 0, 0).astype(LOW)


def attend_back_kernel(
    hidden, middle_grad, attention_grad_low, normed_in, query_proj, key_proj, query_rot, key_rot,
    value_low, prob_low, pre_attention, query_norm, key_norm, cosine, sine, kw, vw,
    q0, q1, q2, q3, o0, o1, o2, o3,
    grad_input, query_keep, query_send, grad_key, grad_value, grad_pre, grad_query_norm,
    grad_key_norm,
):
    cos, sin = cosine[...], sine[...]
    ag = attention_grad_low[...]
    x = normed_in[...]
    k = key_rot[...]
    v = value_low[...]
    scale = k.shape[-1] ** (-0.5)
    key_total = value_total = part = norm_total = None
    for r, (qw, ow) in enumerate(((q0, o0), (q1, o1), (q2, o2), (q3, o3))):
        mg = dot(ag, ow[...], 1, 1).astype(LOW)
        p = prob_low[r]
        pg = dot(mg, v, 1, 1)
        pf = p.astype(F32)
        s = (pf * (pg - jnp.sum(pf * pg, axis=-1, keepdims=True))).astype(LOW)
        qg = dot(s, k) * scale
        kg = dot(s, query_rot[r], 0, 0)
        vg = dot(p, mg, 0, 0)
        qg, gn = norm_back(query_proj[r], query_norm[...], rotate_back(qg, cos, sin))
        qg = qg.astype(LOW)
        out = (query_keep, query_send)[r % 2]
        out[r // 2] = dot(x, qg, 0, 0).astype(LOW)
        ip = dot(qg, qw[...], 1, 1)
        if r == 0:
            key_total, value_total, part, norm_total = kg, vg, ip, gn
        else:
            key_total = key_total + kg
            value_total = value_total + vg
            part = part + ip
            norm_total = norm_total + gn
    grad_query_norm[...] = norm_total
    kg, grad_key_norm[...] = norm_back(
        key_proj[...], key_norm[...], rotate_back(key_total * scale, cos, sin)
    )
    kg = kg.astype(LOW)
    vg = value_total.astype(LOW)
    grad_key[...] = dot(x, kg, 0, 0).astype(LOW)
    grad_value[...] = dot(x, vg, 0, 0).astype(LOW)
    part = part + dot(kg, kw[...], 1, 1) + dot(vg, vw[...], 1, 1)
    back, grad_pre[...] = norm_back(hidden[...].astype(F32), pre_attention[...], part)
    grad_input[...] = (middle_grad[...] + back).astype(LOW)


def swap(array, axis, count, bit):
    return lax.ppermute(array, axis, [(i, i ^ bit) for i in range(count)])


def add_low(a, b):
    return (a.astype(F32) + b.astype(F32)).astype(LOW)


CHUNKS = 5
QUARTER = 384


def plan_steps(groups, rows):
    steps = []
    bit = 1
    while bit < groups:
        halved = rows % 32 == 0
        rows = rows // 2 if halved else rows
        steps.append((bit, halved, rows))
        bit *= 2
    return steps


def reduce_kernel(groups, shapes, *refs):
    refs = list(refs)
    take = lambda n: [refs.pop(0) for _ in range(n)]
    pairs = take(2 * CHUNKS)
    (grad_input,) = take(1)
    outs = take(CHUNKS)
    shared_out, input_out = take(2)
    from_core = take(CHUNKS)
    merged = take(CHUNKS)
    from_second = take(CHUNKS)
    plans = [plan_steps(groups, rows) for rows, _ in shapes]
    halves = [take(len(p)) for p in plans]
    sums = [take(len(p) + 1) for p in plans]
    full = take(CHUNKS)
    shared, inputs, send_sem, recv_sem = take(4)
    me = lax.axis_index("tensor")
    group = lax.axis_index("dp")
    bits = [p[0] for p in plans[0]]
    targets = [{"tensor": me ^ 1}, {"tensor": me ^ 2}] + [{"dp": group ^ bit} for bit in bits]
    barrier = pltpu.get_barrier_semaphore()
    for target in targets:
        pl.semaphore_signal(
            barrier, inc=1, device_id=target, device_id_type=pl.DeviceIdType.MESH
        )
    pl.semaphore_wait(barrier, len(targets))
    started = []

    def send(source, landing, target):
        slot = len(started)
        copy = pltpu.make_async_remote_copy(
            src_ref=source,
            dst_ref=landing,
            send_sem=send_sem.at[slot],
            recv_sem=recv_sem.at[slot],
            device_id=target,
            device_id_type=pl.DeviceIdType.MESH,
        )
        copy.start()
        started.append(copy)
        return copy

    core, second = targets[:2]

    def chunk(c, first):
        rows, columns = shapes[c]
        size = rows * columns / 5e4
        plan = plans[c]
        keep = pairs[2 * c]
        offset = 0
        own = sums[c]
        first.wait_recv()
        merged[c][1] = add_low(keep[1], from_core[c][1])
        copy = send(merged[c].at[1], from_second[c], second)
        merged[c][0] = add_low(keep[0], from_core[c][0])
        yield 0.0
        copy.wait_recv()
        own[0][...] = add_low(merged[c][0], from_second[c][...])
        for i, (bit, halved, count) in enumerate(plan):
            high = (group // bit) % 2
            target = {"dp": group ^ bit}
            if halved:
                mine = pl.ds(pl.multiple_of(high * count, 16), count)
                theirs = pl.ds(pl.multiple_of((1 - high) * count, 16), count)
                offset = offset + high * count
            else:
                mine = theirs = pl.ds(0, count)
            copy = send(own[i].at[theirs], halves[c][i], target)
            yield size * count / rows + 2.0
            copy.wait_recv()
            own[i + 1][...] = add_low(own[i][mine], halves[c][i][...])
        count = plan[-1][2]
        full[c][pl.ds(pl.multiple_of(offset, 16), count)] = own[-1][...]
        for bit, halved, count in reversed(plan):
            if not halved:
                continue
            piece = pl.ds(pl.multiple_of(offset, 16), count)
            copy = send(full[c].at[piece], full[c].at[piece], {"dp": group ^ bit})
            yield size * count / rows + 2.0
            copy.wait_recv()
            offset = offset - (group // bit) % 2 * count
        outs[c][...] = full[c][...]
        if c == CHUNKS - 1:
            shared[me] = full[c][rows - QUARTER :]
            one = send(shared.at[me], shared.at[me], second)
            two = send(shared.at[me], shared.at[me], core)
            yield 4.0
            one.wait_recv()
            three = send(shared.at[me ^ 2], shared.at[me ^ 2], core)
            yield 2.0
            two.wait_recv()
            three.wait_recv()
            for r in range(4):
                shared_out[r] = shared[r]

    order = (4, 0, 1, 2, 3)
    firsts = {c: send(pairs[2 * c + 1], from_core[c], core) for c in order}
    work = [chunk(c, firsts[c]) for c in range(CHUNKS)]
    ready = 3.0
    due = {}
    for c in order:
        next(work[c])
        ready += shapes[c][0] * shapes[c][1] / 2.4e4
        due[c] = ready
        if c == 2:
            inputs[me] = grad_input[...]
    one = send(inputs.at[me], inputs.at[me], second)
    two = send(inputs.at[me], inputs.at[me], core)
    input_due = ready + 14.0
    three = None
    live = set(range(CHUNKS))
    while live or three is None:
        if three is None and (not live or input_due < min(due[c] for c in live)):
            one.wait_recv()
            three = send(inputs.at[me ^ 2], inputs.at[me ^ 2], core)
            continue
        c = min(live, key=lambda i: (due[i], i))
        step = next(work[c], None)
        if step is None:
            live.remove(c)
        else:
            due[c] += step
    two.wait_recv()
    three.wait_recv()
    for r in range(4):
        input_out[r] = inputs[r]
    for copy in started:
        copy.wait_send()


def reduce_all(groups, pairs, grad_input):
    shapes = [keep.shape[1:] for keep, _ in pairs]
    plans = [plan_steps(groups, rows) for rows, _ in shapes]
    args = [a for pair in pairs for a in pair] + [grad_input]
    low = lambda *shape: pltpu.VMEM(shape, LOW)
    outs = [jax.ShapeDtypeStruct(shape, LOW) for shape in shapes]
    outs.append(jax.ShapeDtypeStruct((4, QUARTER, shapes[-1][1]), LOW))
    outs.append(jax.ShapeDtypeStruct((4, *grad_input.shape), LOW))
    scratch = [low(2, *shape) for shape in shapes] * 2 + [low(*shape) for shape in shapes]
    for plan, (_, columns) in zip(plans, shapes):
        scratch += [low(count, columns) for _, _, count in plan]
    for plan, (rows, columns) in zip(plans, shapes):
        scratch += [low(rows, columns)] + [low(count, columns) for _, _, count in plan]
    scratch += [low(*shape) for shape in shapes]
    scratch += [low(*outs[-2].shape), low(*outs[-1].shape)]
    copies = 2 * CHUNKS + 6 + sum(1 + halved for plan in plans for _, halved, _ in plan)
    scratch += [pltpu.SemaphoreType.DMA((copies,))] * 2

    def body(*refs):
        reduce_kernel(groups, shapes, *refs)

    return pl.pallas_call(
        body,
        out_shape=outs,
        in_specs=[pl.BlockSpec(memory_space=pltpu.VMEM)] * len(args),
        out_specs=[pl.BlockSpec(memory_space=pltpu.VMEM)] * len(outs),
        scratch_shapes=scratch,
        compiler_params=pltpu.CompilerParams(
            vmem_limit_bytes=VMEM_LIMIT, collective_id=0, has_side_effects=True
        ),
        cost_estimate=pl.CostEstimate(flops=10**7, bytes_accessed=10**8, transcendentals=0),
    )(*args)


def on_device(groups):
    def run(
        hidden_in, query_weight, key_weight, value_weight, output_weight, gate_weight, up_weight,
        down_weight, pre_attention, query_norm, key_norm, post_attention, pre_feedforward,
        post_feedforward, segments, positions, cotangent,
    ):
        me = lax.axis_index("tensor")
        start = me * LEN
        width, head = key_weight.shape
        units = gate_weight.shape[1]

        shards = [query_weight, output_weight, gate_weight, up_weight, down_weight]
        low_side = lax.axis_index("dp") % 2 == 0

        def second_shard(w):
            half = w.shape[0] // 2
            mine = lax.dynamic_slice_in_dim(w, jnp.where(low_side, 0, half), half, 0)
            mine = swap(mine, "tensor", 4, 2)
            other = swap(mine, "dp", groups, 1)
            return jnp.where(
                low_side,
                jnp.concatenate([mine, other], axis=0),
                jnp.concatenate([other, mine], axis=0),
            )

        seconds = [swap(shards[0], "tensor", 4, 2)] + [second_shard(w) for w in shards[1:]]

        def gathered(i, second):
            w = shards[i]
            return [w, swap(w, "tensor", 4, 1), second, swap(second, "tensor", 4, 1)]

        queries = gathered(0, seconds[0])

        hidden = lax.dynamic_slice_in_dim(hidden_in, start, LEN, 0)
        cot = lax.dynamic_slice_in_dim(cotangent, start, LEN, 0)
        segment = lax.dynamic_slice_in_dim(segments, start, LEN, 0)
        position = lax.dynamic_slice_in_dim(positions, start, LEN, 0)
        steps = jnp.arange(head // 2).astype(F32)
        frequency = jnp.power(F32(ROPE_BASE), -2.0 * steps / head)
        angles = position.astype(F32)[:, None] * frequency[None, :]
        cosine, sine = jnp.cos(angles), jnp.sin(angles)
        row = lambda v: v.reshape(1, -1)
        pre_a, pre_f = row(pre_attention), row(pre_feedforward)
        post_a, post_f = row(post_attention), row(post_feedforward)
        qn, kn = row(query_norm), row(key_norm)

        normed_in, query_proj, key_proj, query_rot, key_rot, value_low, prob_low, mixture = call(
            attend_kernel,
            [
                ((LEN, width), LOW), ((4, LEN, head), F32), ((LEN, head), F32),
                ((4, LEN, head), LOW), ((LEN, head), LOW), ((LEN, head), LOW),
                ((4, LEN, LEN), LOW), ((4, LEN, head), LOW),
            ],
            [
                hidden, pre_a, qn, kn, key_weight, value_weight, *queries, cosine, sine,
                segment[:, None], segment[None, :],
            ],
            4 * 10**9,
        )
        mixture, *seconds = lax.optimization_barrier((mixture, *seconds[1:]))
        outputs = gathered(1, seconds[0])
        attention, middle, normed_mid = call(
            middle_kernel,
            [((LEN, width), F32), ((LEN, width), F32), ((LEN, width), LOW)],
            [hidden, mixture, post_a, pre_f, *outputs],
            10**9,
        )
        normed_mid, *seconds = lax.optimization_barrier((normed_mid, *seconds[1:]))
        gates, ups, downs = [gathered(i + 2, seconds[i]) for i in range(3)]
        args = [attention, middle, normed_mid, cot, post_a, pre_f, post_f, *gates, *ups, *downs]
        outs = [
            ((LEN, width), LOW), ((4, LEN, units), LOW), ((LEN, width), LOW),
            ((4, LEN, units), LOW), ((4, LEN, units), LOW), ((LEN, width), F32),
            ((LEN, width), LOW), ((8, width), F32),
        ]
        (
            hidden_out, product_low, feed_grad_low, gate_grad_low, up_grad_low, middle_grad,
            attention_grad_low, grad_norms,
        ) = pl.pallas_call(
            feed_kernel,
            out_shape=[jax.ShapeDtypeStruct(shape, kind) for shape, kind in outs],
            in_specs=[pl.BlockSpec(memory_space=pltpu.VMEM)] * len(args),
            out_specs=[pl.BlockSpec(memory_space=pltpu.VMEM)] * len(outs),
            scratch_shapes=[pltpu.VMEM((4, LEN, units), F32)] * 2,
            compiler_params=pltpu.CompilerParams(vmem_limit_bytes=VMEM_LIMIT),
            cost_estimate=pl.CostEstimate(
                flops=10**10, bytes_accessed=2 * 10**7, transcendentals=0
            ),
        )(*args)
        hidden_out = lax.all_gather(hidden_out, "tensor", tiled=True)

        def outer(body, a, b, shape):
            return call(body, [((2, *shape), LOW)] * 2, [a, b], 14 * 10**8)

        down = outer(outer_units_kernel, product_low, feed_grad_low, (units, width))
        gate = outer(outer_columns_kernel, normed_mid, gate_grad_low, (width, units))
        up = outer(outer_columns_kernel, normed_mid, up_grad_low, (width, units))
        output = outer(outer_units_kernel, mixture, attention_grad_low, (head, width))
        (
            grad_input, query_keep, query_send, grad_key, grad_value, grad_pre, grad_qn, grad_kn,
        ) = call(
            attend_back_kernel,
            [
                ((LEN, width), LOW), ((2, width, head), LOW), ((2, width, head), LOW),
                ((width, head), LOW), ((width, head), LOW), ((1, width), F32), ((1, head), F32),
                ((1, head), F32),
            ],
            [
                hidden, middle_grad, attention_grad_low, normed_in, query_proj, key_proj,
                query_rot, key_rot, value_low, prob_low, pre_a, qn, kn, cosine, sine, key_weight,
                value_weight, *queries, *outputs,
            ],
            6 * 10**9,
        )
        small = jnp.concatenate(
            [grad_norms[:3].reshape(-1), grad_pre[0], grad_qn[0], grad_kn[0]]
        ).astype(LOW)
        quarter = QUARTER
        small = jnp.pad(small, (0, 256 * head - small.shape[0])).reshape(256, head)
        shared = jnp.concatenate([grad_key, grad_value, small], axis=0)
        parts = [
            lax.dynamic_slice_in_dim(shared, (me ^ r) * quarter, quarter, 0) for r in range(4)
        ]
        keep = jnp.concatenate([query_keep, jnp.stack([parts[0], parts[2]])], axis=1)
        send = jnp.concatenate([query_send, jnp.stack([parts[1], parts[3]])], axis=1)

        *grads, shared, grad_input = reduce_all(
            groups, [down, gate, up, output, (keep, send)], grad_input
        )
        grad_down, grad_gate, grad_up, grad_output = [g.astype(F32) for g in grads[:4]]
        grad_query = grads[4][:width].astype(F32)
        shared = shared.reshape(-1, head).astype(F32)
        grad_input = grad_input.reshape(-1, width).astype(F32)
        small = shared[2 * width :].reshape(-1)
        cuts = [0]
        for size in (width, width, width, width, head, head):
            cuts.append(cuts[-1] + size)
        post_f, pre_f, post_a, pre_a, qn, kn = [
            small[a:b] for a, b in zip(cuts[:-1], cuts[1:])
        ]
        return (
            hidden_out, grad_input, grad_query, shared[:width], shared[width : 2 * width],
            grad_output, grad_gate, grad_up, grad_down, pre_a, qn, kn, post_a, pre_f, post_f,
        )

    return run


def solution(mesh):
    placed = (
        P("dp", None), P(None, "tensor"), P(), P(), P("tensor", None), P(None, "tensor"),
        P(None, "tensor"), P("tensor", None), P(), P(), P(), P(), P(), P(), P("dp"), P("dp"),
        P("dp", None),
    )
    return jax.shard_map(
        on_device(mesh.shape["dp"]),
        mesh=mesh,
        in_specs=placed,
        out_specs=(
            P("dp", None), P("dp", None), P(None, "tensor"), P(), P(), P("tensor", None),
            P(None, "tensor"), P(None, "tensor"), P("tensor", None), P(), P(), P(), P(), P(), P(),
        ),
        check_vma=False,
    )
```
